32 devices in a mesh: dp: 8 (over z, y), tensor: 4 (over x, core).
Axes of the slice: x: 2, y: 2, z: 4, core: 2. Of those that a mesh axis runs over, the one named last changes fastest.
Arguments:
- images: float32 [32, 197, 768], P('dp'), may hold values from -6 to 6
- counts: int32 [8], P('dp'), may hold values from 3 to 4, as said below
- qkv_weight: bfloat16 [2, 768, 3, 12, 64], P(None, 'dp', None, 'tensor'), may hold values from -0.21875 to 0.21875
- qv_bias: bfloat16 [2, 2, 12, 64], P(None, None, 'tensor', 'dp'), may hold values from -4 to 4
- out_weight: bfloat16 [2, 12, 64, 768], P(None, 'tensor', None, 'dp'), may hold values from -0.625 to 0.625
- up_weight: bfloat16 [2, 768, 3072], P(None, 'dp', 'tensor'), may hold values from -0.21875 to 0.21875
- up_bias: bfloat16 [2, 24, 128], P(None, 'tensor', 'dp'), may hold values from -4 to 4
- down_weight: bfloat16 [2, 3072, 768], P(None, 'tensor', 'dp'), may hold values from -0.109375 to 0.109375
- gains: bfloat16 [2, 2, 768], P(None, None, 'dp'), may hold values from 0.099609375 to 1.8984375
- shifts: bfloat16 [2, 4, 768], P(None, None, 'dp'), may hold values from -4 to 4
- cotangent: float32 [32, 197, 768], P('dp'), may hold values from -6 to 6
Outputs:
- activations: float32 [32, 197, 768], P('dp')
- input_grad: float32 [32, 197, 768], P('dp')
- qkv_grad: float32 [2, 768, 3, 12, 64], P(None, 'dp', None, 'tensor')
- qv_bias_grad: float32 [2, 2, 12, 64], P(None, None, 'tensor', 'dp')
- out_grad: float32 [2, 12, 64, 768], P(None, 'tensor', None, 'dp')
- up_grad: float32 [2, 768, 3072], P(None, 'dp', 'tensor')
- up_bias_grad: float32 [2, 24, 128], P(None, 'tensor', 'dp')
- down_grad: float32 [2, 3072, 768], P(None, 'tensor', 'dp')
- gains_grad: float32 [2, 2, 768], P(None, None, 'dp')
- shifts_grad: float32 [2, 4, 768], P(None, None, 'dp')
The draws below stay inside these ranges and needn't reach their ends.
Inputs may be any that keep to these rules, and one draw needn't show every extreme that they name: counts[i] is 3 or 4; in every draw some index holds 4 live images and some index holds 3.
All inputs are finite; a program needn't handle non-finite values.
Results may differ from the reference program's by a relative error of at most 0.0003.
Values may be sent and summed in bfloat16 or wider, within the bound.
A program may use at most 192 MiB of HBM per device.

```python
import math
import jax
import jax.numpy as jnp
from jax import lax

D = 768
HEADS = 12
HD = 64
FF = 3072
SEQ = 197
SLOTS = 4
LAYERS = 2
IMAGES = 32
N_DP = 8


def draw_counts(key, part):
    key = jax.random.fold_in(key, 11)
    first, second, third = jax.random.split(key, 3)
    base = jax.random.randint(first, (N_DP,), SLOTS - 1, SLOTS + 1)
    high_index = jax.random.randint(second, (), 0, N_DP)
    low_index = (high_index + 1 + jax.random.randint(third, (), 0, N_DP - 1)) % N_DP
    places = jnp.arange(N_DP)
    base = jnp.where(places == high_index, SLOTS, base)
    base = jnp.where(places == low_index, SLOTS - 1, base)
    return base.astype(jnp.int32)


def spiked(values, key, source, target, parts, factor):
    def block_of(axis_at):
        return (jnp.arange(values.shape[axis_at]) // (values.shape[axis_at] // parts)).reshape((-1,) + (1,) * (values.ndim - 1 - axis_at))

    first = jax.random.permutation(key, parts)[block_of(target)]
    other_side = (block_of(target) + parts // 2) % parts
    return jnp.where((block_of(source) == first) | (block_of(source) == other_side), factor * values, values)


def level_of(key, extent, shards, smallest, top_value):
    loudness = 1.0
    for axis_at, blocks in shards:
        draws = jax.random.uniform(jax.random.fold_in(jax.random.fold_in(key, 6), axis_at), (blocks,), jnp.float32, smallest / len(shards), top_value / len(shards))
        loudness = loudness * jnp.repeat(jnp.exp(draws), extent[axis_at] // blocks).reshape((-1,) + (1,) * (len(extent) - 1 - axis_at))
    return loudness


def scatter_about(rng, shape, deviation, most, pieces=(), kind=jnp.bfloat16):
    loudness = level_of(rng, shape, pieces, -0.22, 0.18) if pieces else 1.0
    values = jax.random.normal(rng, shape, jnp.float32) * deviation * loudness
    return jnp.minimum(jnp.maximum(values, -most), most).astype(kind)


def gaussian_with(own_key, dims, scale, limit, pieces, heavy, held_as=jnp.bfloat16):
    array = scale * jax.random.normal(own_key, dims, jnp.float32)
    if pieces:
        array = array * level_of(own_key, dims, pieces, -0.22, 0.18)
    return jnp.clip(spiked(array, jax.random.fold_in(own_key, 3), *heavy), -limit, limit).astype(held_as)


def setup_inputs(seed: int = 0) -> dict:
    seeds = jax.random.split(jax.random.key(seed), 12)
    images = scatter_about(seeds[0], (IMAGES, SEQ, D), 1.0, 6.0, ((0, 8),), jnp.float32)
    counts = draw_counts(jax.random.fold_in(seeds[11], 71), 0)
    qkv_weight = scatter_about(seeds[2], (LAYERS, D, 3, HEADS, HD), D ** -0.5, 0.21875, ((1, 8), (3, 4)))
    qv_bias = scatter_about(seeds[3], (LAYERS, 2, HEADS, HD), 0.3, 4.0, ((2, 4), (3, 8)))
    out_weight = scatter_about(seeds[4], (LAYERS, HEADS, HD, D), (D // 8) ** -0.5, 0.625, ((1, 4), (3, 8)))
    up_weight = scatter_about(seeds[5], (LAYERS, D, FF), D ** -0.5, 0.21875, ((1, 8), (2, 4)))
    up_bias = scatter_about(seeds[6], (LAYERS, FF // 128, 128), 0.3, 4.0, ((1, 4), (2, 8)))
    down_weight = scatter_about(seeds[7], (LAYERS, FF, D), FF ** -0.5, 0.109375, ((1, 4), (2, 8)))
    gains = jnp.clip(1.0 + 0.18 * jax.random.normal(seeds[8], (LAYERS, 2, D), jnp.float32), 0.099609375, 1.8984375).astype(jnp.bfloat16)
    shifts = scatter_about(seeds[9], (LAYERS, 4, D), 0.3, 4.0, ((2, 8),))
    cotangent = gaussian_with(seeds[10], (IMAGES, SEQ, D), 1.0, 6.0, ((0, 8),), (0, 2, 8, 2.0), jnp.float32)
    return dict(images=images, counts=counts, qkv_weight=qkv_weight, qv_bias=qv_bias, out_weight=out_weight, up_weight=up_weight, up_bias=up_bias, down_weight=down_weight, gains=gains, shifts=shifts, cotangent=cotangent)


@jax.custom_vjp
def low(v):
    return lax.optimization_barrier(v.astype(jnp.bfloat16)).astype(jnp.float32)

@jax.custom_vjp
def low_back(v):
    return v

def low_keep(v):
    return (low(v), None)

def low_pass(kept, grad):
    return (grad,)

def back_keep(v):
    return (v, None)

def back_low(kept, grad):
    return (low(grad),)
low.defvjp(low_keep, low_pass)
low_back.defvjp(back_keep, back_low)
epsilon = 1e-06
highest = lax.Precision.HIGHEST

def product(a, b):
    return jnp.dot(a, b, precision=highest, preferred_element_type=jnp.float32)

def norm_rows(values, gain, shift):
    average = lax.optimization_barrier(jnp.mean(values, axis=-1, keepdims=True))
    centered = values - average
    variance = lax.optimization_barrier(jnp.mean(centered * centered, axis=-1, keepdims=True))
    return centered * lax.rsqrt(variance + epsilon) * gain + shift

def one_layer(stream, qkv_weight, qv_bias, out_weight, up_weight, up_bias, down_weight, gains, shifts):
    normed = norm_rows(stream, gains[0], shifts[0])
    projected = product(normed, qkv_weight.reshape(D, 3 * D)).reshape(SEQ, 3, HEADS, HD)
    queries = projected[:, 0] + qv_bias[0]
    key_rows = projected[:, 1]
    values = projected[:, 2] + qv_bias[1]
    scores = jnp.einsum('qhe,khe->hqk', queries, key_rows, precision=highest) / math.sqrt(HD)
    weights = jax.nn.softmax(scores, axis=-1)
    mixed = jnp.einsum('hqk,khe->qhe', weights, values, precision=highest).reshape(SEQ, D)
    middle = stream + product(mixed, out_weight.reshape(D, D)) + shifts[2]
    normed_two = norm_rows(middle, gains[1], shifts[1])
    hidden = product(normed_two, up_weight) + up_bias.reshape(FF)
    activated = jax.nn.gelu(hidden, approximate=False)
    return middle + product(activated, down_weight) + shifts[3]

def reference(images, counts, qkv_weight, qv_bias, out_weight, up_weight, up_bias, down_weight, gains, shifts, cotangent):
    params = tuple((p.astype(jnp.float32) for p in (qkv_weight, qv_bias, out_weight, up_weight, up_bias, down_weight, gains, shifts)))
    present = (jnp.arange(SLOTS)[None, :] < counts[:, None]).astype(jnp.float32).reshape(N_DP * SLOTS)

    def forward(stream, weights):
        for layer_index in range(LAYERS):
            stream = one_layer(stream, *[w[layer_index] for w in weights])
        return stream

    def per_image(running, record):
        stream, upstream, alive_flag = record
        result, pullback = jax.vjp(forward, stream, params)
        grad_stream, gradient_set = pullback(upstream * alive_flag)
        running = jax.tree.map(lambda a, b: a + b, running, gradient_set)
        return (running, (result * alive_flag, grad_stream))
    zeros = jax.tree.map(jnp.zeros_like, params)
    totals, (results, grad_images) = lax.scan(per_image, zeros, (images, cotangent, present))
    return (results, grad_images, totals[0], totals[1], totals[2], totals[3], totals[4], totals[5], totals[6], totals[7])
```

```python
import math

import jax
import jax.numpy as jnp
from jax import lax
from jax.sharding import PartitionSpec as P

epsilon = 1e-06
high = lax.Precision.HIGH
f32 = jnp.float32
bf16 = jnp.bfloat16


def weight_product(a, w, w_dim=0):
    top = lax.reduce_precision(a, 8, 7)
    rest = (a - top).astype(bf16)
    dims = (((1,), (w_dim,)), ((), ()))
    return lax.dot_general(
        top.astype(bf16), w, dims, preferred_element_type=f32
    ) + lax.dot_general(rest, w, dims, preferred_element_type=f32)


def cross(a, b):
    return lax.dot_general(
        a, b, (((0,), (0,)), ((), ())), precision=high, preferred_element_type=f32
    )


def heads_product(spec, a, b):
    return jnp.einsum(spec, a, b, precision=high, preferred_element_type=f32)


def norm_keep(values, gain, shift):
    average = jnp.mean(values, axis=-1, keepdims=True)
    centered = values - average
    variance = jnp.mean(centered * centered, axis=-1, keepdims=True)
    inverse = lax.rsqrt(variance + epsilon)
    normed = centered * inverse
    return (normed * gain + shift, normed, inverse)


def norm_back(grad_out, normed, inverse, gain):
    scaled = grad_out * gain
    first_mean = jnp.mean(scaled, axis=-1, keepdims=True)
    second_mean = jnp.mean(scaled * normed, axis=-1, keepdims=True)
    return inverse * (scaled - first_mean - normed * second_mean)


def gelu_parts(hidden):
    normal_cdf = 0.5 * (1.0 + lax.erf(hidden / math.sqrt(2.0)))
    density = jnp.exp(-0.5 * hidden * hidden) / math.sqrt(2.0 * math.pi)
    return (hidden * normal_cdf, normal_cdf + hidden * density)


core_pairs = [(0, 1), (1, 0), (2, 3), (3, 2)]
chip_pairs = [(0, 2), (2, 0), (1, 3), (3, 1)]


def tensor_sum(partial):
    rows, width = partial.shape
    halves = partial.reshape(2, rows // 2, width)
    core = lax.rem(lax.axis_index("tensor"), 2)
    first = core == 0
    mine = jnp.where(first, halves[0], halves[1])
    other = jnp.where(first, halves[1], halves[0])
    mine = mine + lax.ppermute(other, "tensor", core_pairs)
    mine = mine + lax.ppermute(mine, "tensor", chip_pairs)
    other = lax.ppermute(mine, "tensor", core_pairs)
    return jnp.concatenate([jnp.where(first, mine, other), jnp.where(first, other, mine)])


def pack_small(rows_six, bias, up_bias):
    depth = rows_six.shape[1]
    flat = jnp.concatenate([bias.reshape(-1), up_bias.reshape(-1)])
    columns = -(-flat.shape[0] // depth)
    flat = jnp.pad(flat, (0, columns * depth - flat.shape[0])).reshape(columns, depth)
    block = jnp.concatenate([rows_six, flat]).T
    return jnp.pad(block, ((0, 0), (0, 128 - block.shape[1])))


def gather_weights(params, layer):
    qkv, bias, out, up, upb, down, gains, shifts = [p[layer] for p in params]
    depth, heads, head_dim = (qkv.shape[0], qkv.shape[2], qkv.shape[3])
    inner = heads * head_dim
    small = pack_small(jnp.concatenate([gains, shifts]), bias, upb)
    attention = jnp.concatenate(
        [qkv.reshape(depth, 3 * inner), out.reshape(inner, depth).T, small], axis=1
    )
    feed = jnp.concatenate([up, down.T], axis=1)
    attention = lax.all_gather(attention, "dp", axis=0, tiled=True)
    feed = lax.all_gather(feed, "dp", axis=0, tiled=True)
    width = attention.shape[0]
    n = width // depth
    small = attention[:, 4 * inner :].astype(f32).T
    bias_count, upb_count = (bias.size, upb.size)
    columns = -(-(bias_count + upb_count) // depth)
    flat = small[6 : 6 + columns].reshape(columns, n, depth).transpose(1, 0, 2).reshape(n, -1)
    bias_full = (
        flat[:, :bias_count]
        .reshape((n,) + bias.shape)
        .transpose(1, 2, 0, 3)
        .reshape(2, 1, inner)
    )
    upb_full = (
        flat[:, bias_count : bias_count + upb_count]
        .reshape((n,) + upb.shape)
        .transpose(1, 0, 2)
        .reshape(1, -1)
    )
    ff = up.shape[1]
    return dict(
        qkv=attention[:, : 3 * inner],
        out=attention[:, 3 * inner : 4 * inner],
        up=feed[:, :ff],
        down=feed[:, ff:],
        gains=small[:2],
        shifts=small[2:6],
        bias=bias_full,
        upb=upb_full,
        heads=heads,
        head_dim=head_dim,
    )


def layer_forward(stream, w, tokens, padded):
    heads, head_dim = (w["heads"], w["head_dim"])
    inner = heads * head_dim
    rows = stream.shape[0]
    split = (rows // padded, padded, heads, head_dim)
    factor = 1.0 / math.sqrt(head_dim)
    h, normed, inverse = norm_keep(stream, w["gains"][0], w["shifts"][0])
    projected = weight_product(h, w["qkv"])
    q = (projected[:, :inner] + w["bias"][0]).reshape(split)
    k = projected[:, inner : 2 * inner].reshape(split)
    v = (projected[:, 2 * inner :] + w["bias"][1]).reshape(split)
    scores = heads_product("bqhe,bkhe->bhqk", q, k) * factor
    live = lax.broadcasted_iota(jnp.int32, (1, 1, 1, padded), 3) < tokens
    scores = jnp.where(live, scores, -jnp.inf)
    exponent = jnp.exp(scores - jnp.max(scores, axis=-1, keepdims=True))
    soft = exponent / jnp.sum(exponent, axis=-1, keepdims=True)
    mixed = heads_product("bhqk,bkhe->bqhe", soft, v).reshape(rows, inner)
    middle = stream + tensor_sum(weight_product(mixed, w["out"], 1)) + w["shifts"][2]
    h2, normed_two, inverse_two = norm_keep(middle, w["gains"][1], w["shifts"][1])
    hidden = weight_product(h2, w["up"]) + w["upb"]
    activated, slope = gelu_parts(hidden)
    result = middle + tensor_sum(weight_product(activated, w["down"], 1)) + w["shifts"][3]
    return (
        result,
        (normed, inverse, h, q, k, v, soft, mixed, normed_two, inverse_two, h2, activated, slope),
    )


def backward_feed(grad, w, stored):
    normed_two, inverse_two, h2, activated, slope = stored[8:]
    grad_hidden = weight_product(grad, w["down"]) * slope
    grad_norm = tensor_sum(weight_product(grad_hidden, w["up"], 1))
    middle = grad + norm_back(grad_norm, normed_two, inverse_two, w["gains"][1])
    feed = jnp.concatenate([cross(h2, grad_hidden), cross(grad, activated)], axis=1)
    sums = (
        jnp.sum(grad_norm * normed_two, axis=0),
        jnp.sum(grad_norm, axis=0),
        jnp.sum(grad, axis=0),
        jnp.sum(grad_hidden, axis=0),
    )
    return (middle, feed, sums)


def backward_attention(grad, w, stored, padded):
    normed, inverse, h, q, k, v, soft, mixed = stored[:8]
    heads, head_dim = (w["heads"], w["head_dim"])
    inner = heads * head_dim
    rows = grad.shape[0]
    split = (rows // padded, padded, heads, head_dim)
    factor = 1.0 / math.sqrt(head_dim)
    grad_mixed = weight_product(grad, w["out"])
    out_delta = cross(grad, mixed)
    shift_two = jnp.sum(grad, axis=0)
    dots = jnp.sum((grad_mixed * mixed).reshape(split), axis=-1).transpose(0, 2, 1)[..., None]
    grad_mixed = grad_mixed.reshape(split)
    grad_soft = heads_product("bqhe,bkhe->bhqk", grad_mixed, v)
    grad_v = heads_product("bhqk,bqhe->bkhe", soft, grad_mixed).reshape(rows, inner)
    grad_scores = soft * (grad_soft - dots) * factor
    grad_q = heads_product("bhqk,bkhe->bqhe", grad_scores, k).reshape(rows, inner)
    grad_k = heads_product("bhqk,bqhe->bkhe", grad_scores, q).reshape(rows, inner)
    projected = jnp.concatenate([grad_q, grad_k, grad_v], axis=1)
    grad_norm = tensor_sum(weight_product(projected, w["qkv"], 1))
    qkv_delta = cross(h, projected)
    sums = (
        jnp.sum(grad_norm * normed, axis=0),
        jnp.sum(grad_norm, axis=0),
        shift_two,
        jnp.stack([jnp.sum(grad_q, axis=0), jnp.sum(grad_v, axis=0)]),
    )
    grad_in = grad + norm_back(grad_norm, normed, inverse, w["gains"][0])
    return (grad_in, jnp.concatenate([qkv_delta, out_delta], axis=1), sums)


def shards(
    images,
    counts,
    qkv_weight,
    qv_bias,
    out_weight,
    up_weight,
    up_bias,
    down_weight,
    gains,
    shifts,
    cotangent,
):
    params = (qkv_weight, qv_bias, out_weight, up_weight, up_bias, down_weight, gains, shifts)
    slots, tokens, width = images.shape
    layers, depth = qkv_weight.shape[:2]
    n = width // depth
    padded = -(-tokens // 8) * 8
    present = (jnp.arange(slots) < counts[0]).astype(f32)[:, None, None]
    groups = 2
    per = slots // groups
    extend = ((0, 0), (0, padded - tokens), (0, 0))
    x_all = jnp.pad(images, extend)
    g_all = jnp.pad(cotangent * present, extend)
    weights = [gather_weights(params, layer) for layer in range(layers)]
    streams = [x_all[g * per : (g + 1) * per].reshape(per * padded, width) for g in range(groups)]
    grads = [g_all[g * per : (g + 1) * per].reshape(per * padded, width) for g in range(groups)]
    kept = []
    for layer in range(layers):
        both = [layer_forward(s, weights[layer], tokens, padded) for s in streams]
        streams = [b[0] for b in both]
        kept.append([b[1] for b in both])
    totals = [None] * layers
    for layer in reversed(range(layers)):
        w = weights[layer]
        both = [backward_feed(g, w, s) for g, s in zip(grads, kept[layer])]
        feed_total = lax.psum_scatter(
            sum(b[1] for b in both[1:]) + both[0][1], "dp", scatter_dimension=0, tiled=True
        )
        gain_one, shift_one, shift_three, upb_grad = [
            both[0][2][i] + both[1][2][i] for i in range(4)
        ]
        both = [backward_attention(b[0], w, s, padded) for b, s in zip(both, kept[layer])]
        grads = [b[0] for b in both]
        gain_zero, shift_zero, shift_two, bias_grad = [
            both[0][2][i] + both[1][2][i] for i in range(4)
        ]
        six = jnp.stack([gain_zero, gain_one, shift_zero, shift_one, shift_two, shift_three])
        bias_shape = (2, w["heads"], n, w["head_dim"] // n)
        upb_shape = (up_bias.shape[1], n, up_bias.shape[2])
        flat = jnp.concatenate(
            [
                bias_grad.reshape(bias_shape).transpose(2, 0, 1, 3).reshape(n, -1),
                upb_grad.reshape(upb_shape).transpose(1, 0, 2).reshape(n, -1),
            ],
            axis=1,
        )
        columns = -(-flat.shape[1] // depth)
        flat = jnp.pad(flat, ((0, 0), (0, columns * depth - flat.shape[1])))
        flat = flat.reshape(n, columns, depth).transpose(1, 0, 2).reshape(columns, width)
        small = jnp.concatenate([six, flat]).T
        small = jnp.pad(small, ((0, 0), (0, 128 - small.shape[1])))
        attention_total = lax.psum_scatter(
            jnp.concatenate([both[0][1] + both[1][1], small], axis=1),
            "dp",
            scatter_dimension=0,
            tiled=True,
        )
        totals[layer] = (attention_total, feed_total)
    heads, head_dim = qkv_weight.shape[3:]
    inner = heads * head_dim
    ff = up_weight.shape[2]
    collected = []
    for attention, feed in totals:
        small = attention[:, 4 * inner : 4 * inner + 128].T
        bias_count, upb_count = (qv_bias[0].size, up_bias[0].size)
        columns = -(-(bias_count + upb_count) // depth)
        flat = small[6 : 6 + columns].reshape(-1)
        collected.append(
            (
                attention[:, : 3 * inner].reshape(qkv_weight.shape[1:]),
                flat[:bias_count].reshape(qv_bias.shape[1:]),
                attention[:, 3 * inner : 4 * inner].T.reshape(out_weight.shape[1:]),
                feed[:, :ff],
                flat[bias_count : bias_count + upb_count].reshape(up_bias.shape[1:]),
                feed[:, ff:].T,
                small[:2],
                small[2:6],
            )
        )
    joined = [
        jnp.concatenate([s.reshape(per, padded, width) for s in part])[:, :tokens]
        for part in (streams, grads)
    ]
    return (joined[0] * present, joined[1]) + tuple(
        jnp.stack([c[i] for c in collected]) for i in range(8)
    )


def solution(mesh):
    placed = (
        P("dp", None, None),
        P("dp"),
        P(None, "dp", None, "tensor", None),
        P(None, None, "tensor", "dp"),
        P(None, "tensor", None, "dp"),
        P(None, "dp", "tensor"),
        P(None, "tensor", "dp"),
        P(None, "tensor", "dp"),
        P(None, None, "dp"),
        P(None, None, "dp"),
        P("dp", None, None),
    )
    return jax.shard_map(
        shards,
        mesh=mesh,
        in_specs=placed,
        out_specs=(placed[0], placed[0]) + placed[2:10],
        check_vma=False,
    )
```

```python
import math

import jax
import jax.numpy as jnp
from jax import lax
from jax.experimental import pallas as pl
from jax.experimental.pallas import tpu as pltpu
from jax.sharding import PartitionSpec as P

epsilon = 1e-06
high = lax.Precision.HIGH
f32 = jnp.float32
bf16 = jnp.bfloat16


def weight_product(a, w, w_dim=0):
    top = lax.reduce_precision(a, 8, 7)
    rest = (a - top).astype(bf16)
    dims = (((1,), (w_dim,)), ((), ()))
    return lax.dot_general(
        top.astype(bf16), w, dims, preferred_element_type=f32
    ) + lax.dot_general(rest, w, dims, preferred_element_type=f32)


def cross(a, b):
    return lax.dot_general(
        a, b, (((0,), (0,)), ((), ())), precision=high, preferred_element_type=f32
    )


def halves_of(a):
    top = a.astype(bf16)
    return (top, (a - top.astype(f32)).astype(bf16))


def split_dot(a, b, a_dim, b_dim):
    dims = (((a_dim,), (b_dim,)), ((), ()))
    dot = lambda x, y: lax.dot_general(x, y, dims, preferred_element_type=f32)
    return dot(a[0], b[0]) + (dot(a[0], b[1]) + dot(a[1], b[0]))


def soft_of(q, k, factor, tokens):
    scores = split_dot(q, k, 1, 1) * factor
    live = lax.broadcasted_iota(jnp.int32, scores.shape, 1) < tokens
    scores = jnp.where(live, scores, -jnp.inf)
    exponent = jnp.exp(scores - jnp.max(scores, axis=-1, keepdims=True))
    return exponent / jnp.sum(exponent, axis=-1, keepdims=True)


def attention_kernel(heads, head_dim, tokens, x_ref, bias_ref, o_ref):
    inner = heads * head_dim
    factor = 1.0 / math.sqrt(head_dim)
    for j in range(heads):
        at = slice(j * head_dim, (j + 1) * head_dim)
        part = lambda i: x_ref[:, i * inner + j * head_dim : i * inner + (j + 1) * head_dim]
        q = halves_of(part(0) + bias_ref[0:1, at])
        k = halves_of(part(1))
        v = halves_of(part(2) + bias_ref[1:2, at])
        soft = soft_of(q, k, factor, tokens)
        o_ref[:, at] = split_dot(halves_of(soft), v, 1, 0)


def attention_back_kernel(heads, head_dim, tokens, x_ref, bias_ref, o_ref, g_ref, d_ref):
    inner = heads * head_dim
    factor = 1.0 / math.sqrt(head_dim)
    for j in range(heads):
        at = slice(j * head_dim, (j + 1) * head_dim)
        part = lambda i: x_ref[:, i * inner + j * head_dim : i * inner + (j + 1) * head_dim]
        q = halves_of(part(0) + bias_ref[0:1, at])
        k = halves_of(part(1))
        v = halves_of(part(2) + bias_ref[1:2, at])
        soft = soft_of(q, k, factor, tokens)
        grad = g_ref[:, at]
        dots = jnp.sum(grad * o_ref[:, at], axis=-1, keepdims=True)
        grad = halves_of(grad)
        d_soft = split_dot(grad, v, 1, 1)
        d_scores = halves_of(soft * (d_soft - dots) * factor)
        d_ref[:, j * head_dim : (j + 1) * head_dim] = split_dot(d_scores, k, 1, 0)
        d_ref[:, inner + j * head_dim : inner + (j + 1) * head_dim] = split_dot(d_scores, q, 0, 0)
        d_ref[:, 2 * inner + j * head_dim : 2 * inner + (j + 1) * head_dim] = split_dot(
            halves_of(soft), grad, 0, 0
        )


def attention_call(kernel, arrays, bias, width, w, tokens, padded, products):
    rows = arrays[0].shape[0]
    heads, head_dim = (w["heads"], w["head_dim"])
    block = lambda n: pl.BlockSpec((padded, n), lambda i: (i, 0))
    images = rows // padded
    specs = [block(x.shape[1]) for x in arrays]
    specs.insert(1, pl.BlockSpec(bias.shape, lambda i: (0, 0)))
    return pl.pallas_call(
        lambda *refs: kernel(heads, head_dim, tokens, *refs),
        grid=(images,),
        in_specs=specs,
        out_specs=block(width),
        out_shape=jax.ShapeDtypeStruct((rows, width), f32),
        compiler_params=pltpu.CompilerParams(vmem_limit_bytes=32 * 1024 * 1024),
        cost_estimate=pl.CostEstimate(
            flops=products * 6 * images * heads * padded * padded * 2 * head_dim,
            bytes_accessed=4 * rows * (4 * heads * head_dim + width),
            transcendentals=images * heads * padded * padded,
        ),
    )(arrays[0], bias, *arrays[1:])


def norm_keep(values, gain, shift):
    average = jnp.mean(values, axis=-1, keepdims=True)
    centered = values - average
    variance = jnp.mean(centered * centered, axis=-1, keepdims=True)
    inverse = lax.rsqrt(variance + epsilon)
    normed = centered * inverse
    return (normed * gain + shift, normed, inverse)


def norm_back(grad_out, normed, inverse, gain):
    scaled = grad_out * gain
    first_mean = jnp.mean(scaled, axis=-1, keepdims=True)
    second_mean = jnp.mean(scaled * normed, axis=-1, keepdims=True)
    return inverse * (scaled - first_mean - normed * second_mean)


def gelu_parts(hidden):
    normal_cdf = 0.5 * (1.0 + lax.erf(hidden / math.sqrt(2.0)))
    density = jnp.exp(-0.5 * hidden * hidden) / math.sqrt(2.0 * math.pi)
    return (hidden * normal_cdf, normal_cdf + hidden * density)


core_pairs = [(0, 1), (1, 0), (2, 3), (3, 2)]
chip_pairs = [(0, 2), (2, 0), (1, 3), (3, 1)]


def tensor_sum(partial):
    half = partial.shape[0] // 2
    mine = partial[:half] + lax.ppermute(partial[half:], "tensor", core_pairs)
    mine = mine + lax.ppermute(mine, "tensor", chip_pairs)
    return jnp.concatenate([mine, lax.ppermute(mine, "tensor", core_pairs)])


def core_order(rows, first):
    half = rows.shape[0] // 2
    top, rest = (rows[:half], rows[half:])
    return jnp.concatenate([jnp.where(first, top, rest), jnp.where(first, rest, top)])


def pack_small(rows_six, bias, up_bias):
    depth = rows_six.shape[1]
    flat = jnp.concatenate([bias.reshape(-1), up_bias.reshape(-1)])
    columns = -(-flat.shape[0] // depth)
    flat = jnp.pad(flat, (0, columns * depth - flat.shape[0])).reshape(columns, depth)
    block = jnp.concatenate([rows_six, flat]).T
    return jnp.pad(block, ((0, 0), (0, 128 - block.shape[1])))


def gather_weights(params, layer):
    qkv, bias, out, up, upb, down, gains, shifts = [p[layer] for p in params]
    depth, heads, head_dim = (qkv.shape[0], qkv.shape[2], qkv.shape[3])
    inner = heads * head_dim
    small = pack_small(jnp.concatenate([gains, shifts]), bias, upb)
    attention = jnp.concatenate(
        [qkv.reshape(depth, 3 * inner), out.reshape(inner, depth).T, small], axis=1
    )
    feed = jnp.concatenate([up, down.T], axis=1)
    attention = lax.all_gather(attention, "dp", axis=0, tiled=True)
    feed = lax.all_gather(feed, "dp", axis=0, tiled=True)
    width = attention.shape[0]
    n = width // depth
    small = attention[:, 4 * inner :].astype(f32).T
    bias_count, upb_count = (bias.size, upb.size)
    columns = -(-(bias_count + upb_count) // depth)
    flat = small[6 : 6 + columns].reshape(columns, n, depth).transpose(1, 0, 2).reshape(n, -1)
    bias_full = (
        flat[:, :bias_count]
        .reshape((n,) + bias.shape)
        .transpose(1, 2, 0, 3)
        .reshape(2, inner)
    )
    upb_full = (
        flat[:, bias_count : bias_count + upb_count]
        .reshape((n,) + upb.shape)
        .transpose(1, 0, 2)
        .reshape(1, -1)
    )
    ff = up.shape[1]
    return dict(
        qkv=attention[:, : 3 * inner],
        out=attention[:, 3 * inner : 4 * inner],
        up=feed[:, :ff],
        down=feed[:, ff:],
        gains=small[:2],
        shifts=small[2:6],
        bias=bias_full,
        upb=upb_full,
        heads=heads,
        head_dim=head_dim,
    )


def layer_forward(stream, w, tokens, padded):
    heads, head_dim = (w["heads"], w["head_dim"])
    inner = heads * head_dim
    rows = stream.shape[0]
    h, normed, inverse = norm_keep(stream, w["gains"][0], w["shifts"][0])
    projected = weight_product(h, w["qkv"])
    mixed = attention_call(
        attention_kernel, [projected], w["bias"], inner, w, tokens, padded, 2
    )
    middle = stream + tensor_sum(weight_product(mixed, w["out"], 1)) + w["shifts"][2]
    h2, normed_two, inverse_two = norm_keep(middle, w["gains"][1], w["shifts"][1])
    hidden = weight_product(h2, w["up"]) + w["upb"]
    activated, slope = gelu_parts(hidden)
    result = middle + tensor_sum(weight_product(activated, w["down"], 1)) + w["shifts"][3]
    return (
        result,
        (normed, inverse, h, projected, mixed, normed_two, inverse_two, h2, activated, slope),
    )


def backward_feed(grad, w, stored):
    normed_two, inverse_two, h2, activated, slope = stored[5:]
    grad_hidden = weight_product(grad, w["down"]) * slope
    grad_norm = tensor_sum(weight_product(grad_hidden, w["up"], 1))
    middle = grad + norm_back(grad_norm, normed_two, inverse_two, w["gains"][1])
    feed = jnp.concatenate([cross(h2, grad_hidden), cross(grad, activated)], axis=1)
    sums = (
        jnp.sum(grad_norm * normed_two, axis=0),
        jnp.sum(grad_norm, axis=0),
        jnp.sum(grad, axis=0),
        jnp.sum(grad_hidden, axis=0),
    )
    return (middle, feed, sums)


def backward_attention(grad, w, stored, tokens, padded):
    normed, inverse, h, projected, mixed = stored[:5]
    heads, head_dim = (w["heads"], w["head_dim"])
    inner = heads * head_dim
    grad_mixed = weight_product(grad, w["out"])
    out_delta = cross(grad, mixed)
    shift_two = jnp.sum(grad, axis=0)
    projected = attention_call(
        attention_back_kernel,
        [projected, mixed, grad_mixed],
        w["bias"],
        3 * inner,
        w,
        tokens,
        padded,
        5,
    )
    grad_norm = tensor_sum(weight_product(projected, w["qkv"], 1))
    qkv_delta = cross(h, projected)
    sums = (
        jnp.sum(grad_norm * normed, axis=0),
        jnp.sum(grad_norm, axis=0),
        shift_two,
        jnp.sum(projected, axis=0).reshape(3, inner)[::2],
    )
    grad_in = grad + norm_back(grad_norm, normed, inverse, w["gains"][0])
    return (grad_in, jnp.concatenate([qkv_delta, out_delta], axis=1), sums)


def shards(
    images,
    counts,
    qkv_weight,
    qv_bias,
    out_weight,
    up_weight,
    up_bias,
    down_weight,
    gains,
    shifts,
    cotangent,
):
    params = (qkv_weight, qv_bias, out_weight, up_weight, up_bias, down_weight, gains, shifts)
    slots, tokens, width = images.shape
    layers, depth = qkv_weight.shape[:2]
    n = width // depth
    padded = -(-tokens // 8) * 8
    present = (jnp.arange(slots) < counts[0]).astype(f32)[:, None, None]
    groups = 2
    per = slots // groups
    extend = ((0, 0), (0, padded - tokens), (0, 0))
    first = lax.rem(lax.axis_index("tensor"), 2) == 0
    x_all = jnp.pad(images, extend)
    g_all = jnp.pad(cotangent * present, extend)
    weights = [gather_weights(params, layer) for layer in range(layers)]
    streams = [core_order(x_all[g * per : (g + 1) * per], first).reshape(per * padded, width) for g in range(groups)]
    grads = [core_order(g_all[g * per : (g + 1) * per], first).reshape(per * padded, width) for g in range(groups)]
    kept = []
    for layer in range(layers):
        both = [layer_forward(s, weights[layer], tokens, padded) for s in streams]
        streams = [b[0] for b in both]
        kept.append([b[1] for b in both])
    totals = [None] * layers
    for layer in reversed(range(layers)):
        w = weights[layer]
        both = [backward_feed(g, w, s) for g, s in zip(grads, kept[layer])]
        feed, middles = lax.optimization_barrier(
            (both[0][1] + both[1][1], [b[0] for b in both])
        )
        feed_total = lax.psum_scatter(feed, "dp", scatter_dimension=0, tiled=True)
        gain_one, shift_one, shift_three, upb_grad = [
            both[0][2][i] + both[1][2][i] for i in range(4)
        ]
        both = [backward_attention(m, w, s, tokens, padded) for m, s in zip(middles, kept[layer])]
        grads = [b[0] for b in both]
        gain_zero, shift_zero, shift_two, bias_grad = [
            both[0][2][i] + both[1][2][i] for i in range(4)
        ]
        six = jnp.stack([gain_zero, gain_one, shift_zero, shift_one, shift_two, shift_three])
        bias_shape = (2, w["heads"], n, w["head_dim"] // n)
        upb_shape = (up_bias.shape[1], n, up_bias.shape[2])
        flat = jnp.concatenate(
            [
                bias_grad.reshape(bias_shape).transpose(2, 0, 1, 3).reshape(n, -1),
                upb_grad.reshape(upb_shape).transpose(1, 0, 2).reshape(n, -1),
            ],
            axis=1,
        )
        columns = -(-flat.shape[1] // depth)
        flat = jnp.pad(flat, ((0, 0), (0, columns * depth - flat.shape[1])))
        flat = flat.reshape(n, columns, depth).transpose(1, 0, 2).reshape(columns, width)
        small = jnp.concatenate([six, flat]).T
        small = jnp.pad(small, ((0, 0), (0, 128 - small.shape[1])))
        attention_total = lax.psum_scatter(
            jnp.concatenate([both[0][1] + both[1][1], small], axis=1),
            "dp",
            scatter_dimension=0,
            tiled=True,
        )
        totals[layer] = (attention_total, feed_total)
    heads, head_dim = qkv_weight.shape[3:]
    inner = heads * head_dim
    ff = up_weight.shape[2]
    collected = []
    for attention, feed in totals:
        small = attention[:, 4 * inner : 4 * inner + 128].T
        bias_count, upb_count = (qv_bias[0].size, up_bias[0].size)
        columns = -(-(bias_count + upb_count) // depth)
        flat = small[6 : 6 + columns].reshape(-1)
        collected.append(
            (
                attention[:, : 3 * inner].reshape(qkv_weight.shape[1:]),
                flat[:bias_count].reshape(qv_bias.shape[1:]),
                attention[:, 3 * inner : 4 * inner].T.reshape(out_weight.shape[1:]),
                feed[:, :ff],
                flat[bias_count : bias_count + upb_count].reshape(up_bias.shape[1:]),
                feed[:, ff:].T,
                small[:2],
                small[2:6],
            )
        )
    joined = [
        jnp.concatenate([core_order(s.reshape(per, padded, width), first) for s in part])[:, :tokens]
        for part in (streams, grads)
    ]
    return (joined[0] * present, joined[1]) + tuple(
        jnp.stack([c[i] for c in collected]) for i in range(8)
    )


def solution(mesh):
    placed = (
        P("dp", None, None),
        P("dp"),
        P(None, "dp", None, "tensor", None),
        P(None, None, "tensor", "dp"),
        P(None, "tensor", None, "dp"),
        P(None, "dp", "tensor"),
        P(None, "tensor", "dp"),
        P(None, "tensor", "dp"),
        P(None, None, "dp"),
        P(None, None, "dp"),
        P("dp", None, None),
    )
    return jax.shard_map(
        shards,
        mesh=mesh,
        in_specs=placed,
        out_specs=(placed[0], placed[0]) + placed[2:10],
        check_vma=False,
    )
```

```python
import math

import jax
import jax.numpy as jnp
from jax import lax
from jax.experimental import pallas as pl
from jax.experimental.pallas import tpu as pltpu
from jax.sharding import PartitionSpec as P

epsilon = 1e-06
high = lax.Precision.HIGH
f32 = jnp.float32
bf16 = jnp.bfloat16


def weight_product(a, w, w_dim=0):
    top = lax.reduce_precision(a, 8, 7)
    rest = (a - top).astype(bf16)
    dims = (((1,), (w_dim,)), ((), ()))
    return lax.dot_general(
        top.astype(bf16), w, dims, preferred_element_type=f32
    ) + lax.dot_general(rest, w, dims, preferred_element_type=f32)


def cross(a, b):
    return lax.dot_general(
        a, b, (((0,), (0,)), ((), ())), precision=high, preferred_element_type=f32
    )


def halves_of(a):
    top = a.astype(bf16)
    return (top, (a - top.astype(f32)).astype(bf16))


def split_dot(a, b, a_dim, b_dim):
    dims = (((a_dim,), (b_dim,)), ((), ()))
    dot = lambda x, y: lax.dot_general(x, y, dims, preferred_element_type=f32)
    return dot(a[0], b[0]) + (dot(a[0], b[1]) + dot(a[1], b[0]))


def soft_of(q, k, factor, tokens):
    scores = split_dot(q, k, 1, 1) * factor
    live = lax.broadcasted_iota(jnp.int32, scores.shape, 1) < tokens
    scores = jnp.where(live, scores, -jnp.inf)
    exponent = jnp.exp(scores - jnp.max(scores, axis=-1, keepdims=True))
    return exponent / jnp.sum(exponent, axis=-1, keepdims=True)


def attention_kernel(heads, head_dim, tokens, x_ref, bias_ref, o_ref):
    inner = heads * head_dim
    factor = 1.0 / math.sqrt(head_dim)
    for j in range(heads):
        at = slice(j * head_dim, (j + 1) * head_dim)
        part = lambda i: x_ref[:, i * inner + j * head_dim : i * inner + (j + 1) * head_dim]
        q = halves_of(part(0) + bias_ref[0:1, at])
        k = halves_of(part(1))
        v = halves_of(part(2) + bias_ref[1:2, at])
        soft = soft_of(q, k, factor, tokens)
        o_ref[:, at] = split_dot(halves_of(soft), v, 1, 0)


def attention_back_kernel(heads, head_dim, tokens, x_ref, bias_ref, o_ref, g_ref, d_ref):
    inner = heads * head_dim
    factor = 1.0 / math.sqrt(head_dim)
    for j in range(heads):
        at = slice(j * head_dim, (j + 1) * head_dim)
        part = lambda i: x_ref[:, i * inner + j * head_dim : i * inner + (j + 1) * head_dim]
        q = halves_of(part(0) + bias_ref[0:1, at])
        k = halves_of(part(1))
        v = halves_of(part(2) + bias_ref[1:2, at])
        soft = soft_of(q, k, factor, tokens)
        grad = g_ref[:, at]
        dots = jnp.sum(grad * o_ref[:, at], axis=-1, keepdims=True)
        grad = halves_of(grad)
        d_soft = split_dot(grad, v, 1, 1)
        d_scores = halves_of(soft * (d_soft - dots) * factor)
        d_ref[:, j * head_dim : (j + 1) * head_dim] = split_dot(d_scores, k, 1, 0)
        d_ref[:, inner + j * head_dim : inner + (j + 1) * head_dim] = split_dot(d_scores, q, 0, 0)
        d_ref[:, 2 * inner + j * head_dim : 2 * inner + (j + 1) * head_dim] = split_dot(
            halves_of(soft), grad, 0, 0
        )


def attention_call(kernel, arrays, bias, width, w, tokens, padded, products):
    rows = arrays[0].shape[0]
    heads, head_dim = (w["heads"], w["head_dim"])
    block = lambda n: pl.BlockSpec((padded, n), lambda i: (i, 0))
    images = rows // padded
    specs = [block(x.shape[1]) for x in arrays]
    specs.insert(1, pl.BlockSpec(bias.shape, lambda i: (0, 0)))
    return pl.pallas_call(
        lambda *refs: kernel(heads, head_dim, tokens, *refs),
        grid=(images,),
        in_specs=specs,
        out_specs=block(width),
        out_shape=jax.ShapeDtypeStruct((rows, width), f32),
        compiler_params=pltpu.CompilerParams(vmem_limit_bytes=32 * 1024 * 1024),
        cost_estimate=pl.CostEstimate(
            flops=products * 6 * images * heads * padded * padded * 2 * head_dim,
            bytes_accessed=4 * rows * (4 * heads * head_dim + width),
            transcendentals=images * heads * padded * padded,
        ),
    )(arrays[0], bias, *arrays[1:])


def norm_keep(values, gain, shift):
    average = jnp.mean(values, axis=-1, keepdims=True)
    centered = values - average
    variance = jnp.mean(centered * centered, axis=-1, keepdims=True)
    inverse = lax.rsqrt(variance + epsilon)
    normed = centered * inverse
    return (normed * gain + shift, normed, inverse)


def norm_back(grad_out, normed, inverse, gain):
    scaled = grad_out * gain
    first_mean = jnp.mean(scaled, axis=-1, keepdims=True)
    second_mean = jnp.mean(scaled * normed, axis=-1, keepdims=True)
    return inverse * (scaled - first_mean - normed * second_mean)


def gelu_parts(hidden):
    normal_cdf = 0.5 * (1.0 + lax.erf(hidden / math.sqrt(2.0)))
    density = jnp.exp(-0.5 * hidden * hidden) / math.sqrt(2.0 * math.pi)
    return (hidden * normal_cdf, normal_cdf + hidden * density)


core_pairs = [(0, 1), (1, 0), (2, 3), (3, 2)]
chip_pairs = [(0, 2), (2, 0), (1, 3), (3, 1)]


def tensor_sum(partial):
    half = partial.shape[0] // 2
    mine = partial[:half] + lax.ppermute(partial[half:], "tensor", core_pairs)
    mine = mine + lax.ppermute(mine, "tensor", chip_pairs)
    return jnp.concatenate([mine, lax.ppermute(mine, "tensor", core_pairs)])


def core_order(rows, first):
    half = rows.shape[0] // 2
    top, rest = (rows[:half], rows[half:])
    return jnp.concatenate([jnp.where(first, top, rest), jnp.where(first, rest, top)])


def pack_small(rows_six, bias, up_bias):
    depth = rows_six.shape[1]
    flat = jnp.concatenate([bias.reshape(-1), up_bias.reshape(-1)])
    columns = -(-flat.shape[0] // depth)
    flat = jnp.pad(flat, (0, columns * depth - flat.shape[0])).reshape(columns, depth)
    block = jnp.concatenate([rows_six, flat]).T
    return jnp.pad(block, ((0, 0), (0, 128 - block.shape[1])))


def gather_weights(params, layer):
    qkv, bias, out, up, upb, down, gains, shifts = [p[layer] for p in params]
    depth, heads, head_dim = (qkv.shape[0], qkv.shape[2], qkv.shape[3])
    inner = heads * head_dim
    small = pack_small(jnp.concatenate([gains, shifts]), bias, upb)
    attention = jnp.concatenate(
        [qkv.reshape(depth, 3 * inner), out.reshape(inner, depth).T, small], axis=1
    )
    feed = jnp.concatenate([up, down.T], axis=1)
    attention = lax.all_gather(attention, "dp", axis=0, tiled=True)
    feed = lax.all_gather(feed, "dp", axis=0, tiled=True)
    width = attention.shape[0]
    n = width // depth
    small = attention[:, 4 * inner :].astype(f32).T
    bias_count, upb_count = (bias.size, upb.size)
    columns = -(-(bias_count + upb_count) // depth)
    flat = small[6 : 6 + columns].reshape(columns, n, depth).transpose(1, 0, 2).reshape(n, -1)
    bias_full = (
        flat[:, :bias_count]
        .reshape((n,) + bias.shape)
        .transpose(1, 2, 0, 3)
        .reshape(2, inner)
    )
    upb_full = (
        flat[:, bias_count : bias_count + upb_count]
        .reshape((n,) + upb.shape)
        .transpose(1, 0, 2)
        .reshape(1, -1)
    )
    ff = up.shape[1]
    return dict(
        qkv=attention[:, : 3 * inner],
        out=attention[:, 3 * inner : 4 * inner],
        up=feed[:, :ff],
        down=feed[:, ff:],
        gains=small[:2],
        shifts=small[2:6],
        bias=bias_full,
        upb=upb_full,
        heads=heads,
        head_dim=head_dim,
    )


def layer_forward(stream, w, tokens, padded):
    heads, head_dim = (w["heads"], w["head_dim"])
    inner = heads * head_dim
    rows = stream.shape[0]
    h, normed, inverse = norm_keep(stream, w["gains"][0], w["shifts"][0])
    projected = weight_product(h, w["qkv"])
    mixed = attention_call(
        attention_kernel, [projected], w["bias"], inner, w, tokens, padded, 2
    )
    middle = stream + tensor_sum(weight_product(mixed, w["out"], 1)) + w["shifts"][2]
    h2, normed_two, inverse_two = norm_keep(middle, w["gains"][1], w["shifts"][1])
    hidden = weight_product(h2, w["up"]) + w["upb"]
    activated, slope = gelu_parts(hidden)
    result = middle + tensor_sum(weight_product(activated, w["down"], 1)) + w["shifts"][3]
    return (
        result,
        (normed, inverse, h, projected, mixed, normed_two, inverse_two, h2, activated, slope),
    )


def backward_feed(grad, w, stored):
    normed_two, inverse_two, h2, activated, slope = stored[5:]
    grad_hidden = weight_product(grad, w["down"]) * slope
    grad_norm = tensor_sum(weight_product(grad_hidden, w["up"], 1))
    middle = grad + norm_back(grad_norm, normed_two, inverse_two, w["gains"][1])
    feed = jnp.concatenate([cross(h2, grad_hidden), cross(grad, activated)], axis=1)
    sums = (
        jnp.sum(grad_norm * normed_two, axis=0),
        jnp.sum(grad_norm, axis=0),
        jnp.sum(grad, axis=0),
        jnp.sum(grad_hidden, axis=0),
    )
    return (middle, feed, sums)


def backward_attention(grad, w, stored, tokens, padded):
    normed, inverse, h, projected, mixed = stored[:5]
    heads, head_dim = (w["heads"], w["head_dim"])
    inner = heads * head_dim
    grad_mixed = weight_product(grad, w["out"])
    out_delta = cross(grad, mixed)
    shift_two = jnp.sum(grad, axis=0)
    projected = attention_call(
        attention_back_kernel,
        [projected, mixed, grad_mixed],
        w["bias"],
        3 * inner,
        w,
        tokens,
        padded,
        5,
    )
    grad_norm = tensor_sum(weight_product(projected, w["qkv"], 1))
    qkv_delta = cross(h, projected)
    sums = (
        jnp.sum(grad_norm * normed, axis=0),
        jnp.sum(grad_norm, axis=0),
        shift_two,
        jnp.sum(projected, axis=0).reshape(3, inner)[::2],
    )
    grad_in = grad + norm_back(grad_norm, normed, inverse, w["gains"][0])
    return (grad_in, jnp.concatenate([qkv_delta, out_delta], axis=1), sums)


def shards(
    images,
    counts,
    qkv_weight,
    qv_bias,
    out_weight,
    up_weight,
    up_bias,
    down_weight,
    gains,
    shifts,
    cotangent,
):
    params = (qkv_weight, qv_bias, out_weight, up_weight, up_bias, down_weight, gains, shifts)
    slots, tokens, width = images.shape
    layers, depth = qkv_weight.shape[:2]
    n = width // depth
    padded = -(-tokens // 8) * 8
    present = (jnp.arange(slots) < counts[0]).astype(f32)[:, None, None]
    groups = 2
    per = slots // groups
    extend = ((0, 0), (0, padded - tokens), (0, 0))
    first = lax.rem(lax.axis_index("tensor"), 2) == 0
    x_all = jnp.pad(images, extend)
    g_all = jnp.pad(cotangent * present, extend)
    weights = [gather_weights(params, layer) for layer in range(layers)]
    streams = [core_order(x_all[g * per : (g + 1) * per], first).reshape(per * padded, width) for g in range(groups)]
    grads = [core_order(g_all[g * per : (g + 1) * per], first).reshape(per * padded, width) for g in range(groups)]
    kept = []
    for layer in range(layers):
        both = [layer_forward(s, weights[layer], tokens, padded) for s in streams]
        streams = [b[0] for b in both]
        kept.append([b[1] for b in both])
    totals = [None] * layers
    for layer in reversed(range(layers)):
        w = weights[layer]
        both = [backward_feed(g, w, s) for g, s in zip(grads, kept[layer])]
        feed, middles = lax.optimization_barrier(
            (both[0][1] + both[1][1], [b[0] for b in both])
        )
        feed_total = lax.psum_scatter(feed, "dp", scatter_dimension=0, tiled=True)
        gain_one, shift_one, shift_three, upb_grad = [
            both[0][2][i] + both[1][2][i] for i in range(4)
        ]
        both = [backward_attention(m, w, s, tokens, padded) for m, s in zip(middles, kept[layer])]
        grads = [b[0] for b in both]
        gain_zero, shift_zero, shift_two, bias_grad = [
            both[0][2][i] + both[1][2][i] for i in range(4)
        ]
        six = jnp.stack([gain_zero, gain_one, shift_zero, shift_one, shift_two, shift_three])
        bias_shape = (2, w["heads"], n, w["head_dim"] // n)
        upb_shape = (up_bias.shape[1], n, up_bias.shape[2])
        flat = jnp.concatenate(
            [
                bias_grad.reshape(bias_shape).transpose(2, 0, 1, 3).reshape(n, -1),
                upb_grad.reshape(upb_shape).transpose(1, 0, 2).reshape(n, -1),
            ],
            axis=1,
        )
        columns = -(-flat.shape[1] // depth)
        flat = jnp.pad(flat, ((0, 0), (0, columns * depth - flat.shape[1])))
        flat = flat.reshape(n, columns, depth).transpose(1, 0, 2).reshape(columns, width)
        filler = jnp.tile(feed_total[:, :1], (n, 1))
        small = jnp.concatenate([jnp.concatenate([six, flat]).T, filler], axis=1)
        small = jnp.pad(small, ((0, 0), (0, 128 - small.shape[1])))
        attention_total = lax.psum_scatter(
            jnp.concatenate([both[0][1] + both[1][1], small], axis=1),
            "dp",
            scatter_dimension=0,
            tiled=True,
        )
        totals[layer] = (attention_total, feed_total)
    heads, head_dim = qkv_weight.shape[3:]
    inner = heads * head_dim
    ff = up_weight.shape[2]
    collected = []
    for attention, feed in totals:
        small = attention[:, 4 * inner : 4 * inner + 128].T
        bias_count, upb_count = (qv_bias[0].size, up_bias[0].size)
        columns = -(-(bias_count + upb_count) // depth)
        flat = small[6 : 6 + columns].reshape(-1)
        collected.append(
            (
                attention[:, : 3 * inner].reshape(qkv_weight.shape[1:]),
                flat[:bias_count].reshape(qv_bias.shape[1:]),
                attention[:, 3 * inner : 4 * inner].T.reshape(out_weight.shape[1:]),
                feed[:, :ff],
                flat[bias_count : bias_count + upb_count].reshape(up_bias.shape[1:]),
                feed[:, ff:].T,
                small[:2],
                small[2:6],
            )
        )
    joined = [
        jnp.concatenate([core_order(s.reshape(per, padded, width), first) for s in part])[:, :tokens]
        for part in (streams, grads)
    ]
    return (joined[0] * present, joined[1]) + tuple(
        jnp.stack([c[i] for c in collected]) for i in range(8)
    )


def solution(mesh):
    placed = (
        P("dp", None, None),
        P("dp"),
        P(None, "dp", None, "tensor", None),
        P(None, None, "tensor", "dp"),
        P(None, "tensor", None, "dp"),
        P(None, "dp", "tensor"),
        P(None, "tensor", "dp"),
        P(None, "tensor", "dp"),
        P(None, None, "dp"),
        P(None, None, "dp"),
        P("dp", None, None),
    )
    return jax.shard_map(
        shards,
        mesh=mesh,
        in_specs=placed,
        out_specs=(placed[0], placed[0]) + placed[2:10],
        check_vma=False,
    )
```
